256 devices in a mesh: row: 16 (over y, z_lo), col: 16 (over z_hi, x, core).
Axes of the slice: x: 4, y: 4, z: 8 (z_hi: 2, z_lo: 4; z = z_hi * 4 + z_lo), core: 2. Of those that a mesh axis runs over, the one named last changes fastest.
Arguments:
- student: bfloat16 [8192, 2048], P(('row', 'col')), may hold values from -0.125 to 0.125
- teacher: bfloat16 [8192, 4096], P(('row', 'col')), may hold values from -0.09375 to 0.09375
Outputs:
- distance: float32 [], replicated
- student_grad: float32 [8192, 2048], P(('row', 'col'))
The draws below stay inside these ranges and needn't reach their ends.
All inputs are finite; a program needn't handle non-finite values.
Results may differ from the reference program's by a relative error of at most 0.0015.
Values may be sent and summed in bfloat16 or wider, within the bound.
No kernel may reach another device: no remote copies, remote signals or barrier semaphores. Data moves between devices by JAX's collectives and lax.ppermute only.
A program may use at most 64 MiB of HBM per device.

```python
import math
import jax
import jax.numpy as jnp
from jax import lax

DS = 2048
DT = 4096
N = 8192


def block_levels(stream_key, dims, split, least, high):
    def one(axis_at, blocks):
        heights = jax.random.uniform(jax.random.fold_in(jax.random.fold_in(stream_key, 6), axis_at), (blocks,), jnp.float32, least / len(split), high / len(split))
        return jnp.repeat(jnp.exp(heights), dims[axis_at] // blocks).reshape((-1,) + (1,) * (len(dims) - axis_at - 1))

    loudness = one(*split[0])
    for cut in split[1:]:
        loudness = loudness * one(*cut)
    return loudness


def bell_draw(own_key, shape, spread, bound, cuts=(), held_as=jnp.bfloat16):
    entries = spread * jax.random.normal(own_key, shape, jnp.float32)
    if cuts:
        entries = entries * block_levels(own_key, shape, cuts, -0.22, 0.18)
    return jnp.clip(entries, -bound, bound).astype(held_as)


def setup_inputs(seed: int = 0) -> dict:
    arg_keys = jax.random.split(jax.random.key(seed), 3)
    return {
        "student": bell_draw(arg_keys[0], (N, DS), DS ** -0.5, 0.125, ((0, 256),)),
        "teacher": bell_draw(arg_keys[1], (N, DT), DT ** -0.5, 0.09375, ((0, 256),)),
    }


def reference(student, teacher):
    height = math.gcd(N, 1024)
    starts = jnp.arange(N // height, dtype=jnp.int32) * height

    def block_terms(start):
        s_block = lax.dynamic_slice_in_dim(student, start, height, 0)
        t_block = lax.dynamic_slice_in_dim(teacher, start, height, 0)
        gram_s = jnp.dot(s_block, student.T, preferred_element_type=jnp.float32)
        gram_t = jnp.dot(t_block, teacher.T, preferred_element_type=jnp.float32)
        excess = gram_s - gram_t
        rounded = excess.astype(jnp.bfloat16)
        pulled = jnp.dot(rounded, student, preferred_element_type=jnp.float32)
        return pulled, jnp.sum(excess * excess)

    pulled, squares = lax.map(block_terms, starts)
    distance = jnp.sum(squares) / jnp.float32(N)
    return distance, pulled.reshape(N, DS)
```

```python
import jax
import jax.numpy as jnp
from jax import lax
from jax.sharding import Mesh, PartitionSpec as P

AXES = ("y", "zl", "zh", "x", "core")
SIZES = (4, 4, 2, 4, 2)
STRIDES = (64, 16, 8, 2, 1)


def shift(value, **steps):
    pairs = []
    for target in range(256):
        source = 0
        for axis, size, stride in zip(AXES, SIZES, STRIDES):
            source += (target // stride + steps.get(axis, 0)) % size * stride
        pairs.append((source, target))
    return lax.ppermute(value, AXES, pairs)


def shards(student, teacher):
    texts, width = student.shape
    rows = lax.all_gather(
        jnp.concatenate([student, -teacher], axis=1), ("zh", "zl", "core"), axis=0, tiled=True
    )
    both = jnp.concatenate([student, teacher], axis=1)
    half = texts // 2
    upper, lower = both[:half], both[half:]
    upper = jnp.concatenate([upper] + [shift(upper, x=k) for k in (1, 3, 2)])
    lower = jnp.concatenate([lower] + [shift(lower, y=k) for k in (1, 3, 2)])
    cols = jnp.concatenate(
        [upper, lower]
        + [f for k in (1, 3, 2) for f in (shift(upper, y=k), shift(lower, x=k))]
    )
    excess = lax.dot_general(
        rows, cols, (((1,), (1,)), ((), ())), preferred_element_type=jnp.float32
    )
    squares = jnp.sum(excess * excess)
    rounded = excess.astype(jnp.bfloat16).reshape(8, 2, texts, -1)
    cols_s = cols[:, :width]
    core = lax.axis_index("core")

    def pull(which):
        picked = lax.dynamic_index_in_dim(rounded, which, 1, keepdims=False)
        return jnp.dot(
            picked.reshape(8 * texts, -1), cols_s, preferred_element_type=jnp.float32
        )

    other = shift(pull(1 - core), core=1)
    partial_term = pull(core) + other
    pulled = lax.psum_scatter(partial_term, ("zh", "zl"), scatter_dimension=0, tiled=True)

    plane = lax.all_to_all(
        jnp.broadcast_to(squares, (32, 8, 128)), ("y", "x", "core"), 0, 0
    )
    plane = jnp.sum(plane[:, 0, 0])
    line = lax.all_to_all(jnp.broadcast_to(plane, (8, 8, 128)), ("zh", "zl"), 0, 0)
    distance = jnp.sum(line[:, 0, 0]) / jnp.float32(texts * 256)
    return distance, pulled


def solution(mesh):
    fine = Mesh(mesh.devices.reshape(SIZES), AXES)
    spec = P(AXES, None)
    return jax.shard_map(
        shards, mesh=fine, in_specs=(spec, spec), out_specs=(P(), spec), check_vma=False
    )
```

```python
import jax
import jax.numpy as jnp
from jax import lax
from jax.experimental import pallas as pl
from jax.experimental.pallas import tpu as pltpu
from jax.sharding import Mesh, PartitionSpec as P

AXES = ("y", "zl", "zh", "x", "core")
SIZES = (4, 4, 2, 4, 2)
STRIDES = (64, 16, 8, 2, 1)
NEAR = (1, 3, 2)
DEPTH = 1024


def shift(value, **steps):
    pairs = []
    for target in range(256):
        source = 0
        for axis, size, stride in zip(AXES, SIZES, STRIDES):
            source += (target // stride + steps.get(axis, 0)) % size * stride
        pairs.append((source, target))
    return lax.ppermute(value, AXES, pairs)


def join_kernel(student_ref, teacher_ref, both_ref, upper_ref, lower_ref):
    width = student_ref.shape[1]
    half = upper_ref.shape[0]
    for source, place in ((student_ref, slice(0, width)), (teacher_ref, slice(width, None))):
        both_ref[:, place] = source[...]
        upper_ref[:, place] = source[:half]
        lower_ref[:, place] = source[half:]


def join(student, teacher):
    texts, total = student.shape[0], student.shape[1] + teacher.shape[1]
    whole = jax.ShapeDtypeStruct((texts, total), student.dtype)
    part = jax.ShapeDtypeStruct((texts // 2, total), student.dtype)
    return pl.pallas_call(join_kernel, out_shape=(whole, part, part))(student, teacher)


def excess_kernel(student_steps, *refs):
    *pieces, rows_ref, rounded_ref, squares_ref, total = refs
    step = pl.program_id(0)
    cols = jnp.concatenate([piece[...] for piece in pieces])
    product = lax.dot_general(
        cols, rows_ref[...], (((1,), (1,)), ((), ())), preferred_element_type=jnp.float32
    )

    @pl.when(step == 0)
    def _():
        total[...] = product

    @pl.when((step > 0) & (step < student_steps))
    def _():
        total[...] += product

    @pl.when(step >= student_steps)
    def _():
        total[...] -= product

    @pl.when(step == pl.num_programs(0) - 1)
    def _():
        excess = total[...]
        rounded_ref[...] = excess.astype(rounded_ref.dtype)
        squares = jnp.sum(jnp.sum(excess * excess, axis=0, keepdims=True), axis=1, keepdims=True)
        squares_ref[...] = jnp.broadcast_to(squares, squares_ref.shape)


def excess_of(pieces, rows, student_width):
    texts, width = rows.shape
    count = sum(piece.shape[0] for piece in pieces)
    block = lambda height: pl.BlockSpec((height, DEPTH), lambda k: (0, k))
    fixed = lambda *shape: pl.BlockSpec(shape, lambda k: (0,) * len(shape))
    return pl.pallas_call(
        lambda *refs: excess_kernel(student_width // DEPTH, *refs),
        grid=(width // DEPTH,),
        in_specs=[block(piece.shape[0]) for piece in pieces] + [block(texts)],
        out_specs=(fixed(count, texts), fixed(8, 128)),
        out_shape=(
            jax.ShapeDtypeStruct((count, texts), jnp.bfloat16),
            jax.ShapeDtypeStruct((8, 128), jnp.float32),
        ),
        scratch_shapes=[pltpu.VMEM((count, texts), jnp.float32)],
        compiler_params=pltpu.CompilerParams(vmem_limit_bytes=32 * 1024 * 1024),
        cost_estimate=pl.CostEstimate(
            flops=2 * count * texts * width,
            bytes_accessed=2 * (count + texts) * width,
            transcendentals=0,
        ),
    )(*pieces, rows)


def shards(student, teacher):
    texts, width = student.shape
    half = texts // 2
    both, upper, lower = join(student, teacher)
    rows = lax.all_gather(both, ("zh", "zl", "core"), axis=0, tiled=True)
    upper = jnp.concatenate([upper] + [shift(upper, x=k) for k in NEAR])
    lower = jnp.concatenate([lower] + [shift(lower, y=k) for k in NEAR])
    pieces = []
    for k in NEAR:
        pieces += [shift(upper, y=k), shift(lower, x=k)]
    pieces += [upper, lower]
    rounded, squares = excess_of(pieces, rows, width)
    rows_s = rows[:, :width]
    bundle = 4 * half
    pull = lambda start, count: jnp.dot(
        rounded[start * bundle : (start + count) * bundle],
        rows_s,
        preferred_element_type=jnp.float32,
    ).reshape(count, 4, half, width)
    sent = pull(0, 6)
    own = pull(6, 2)
    upper_sum, lower_sum = own[0], own[1]
    for i, k in enumerate(NEAR):
        back = shift(sent[2 * i], y=-k)
        if i == 0:
            back, squares = lax.optimization_barrier((back, squares))
        upper_sum += back
        lower_sum += shift(sent[2 * i + 1], x=-k)
    upper_grad, lower_grad = upper_sum[0], lower_sum[0]
    for i, k in enumerate(NEAR):
        upper_grad += shift(upper_sum[i + 1], x=-k)
        lower_grad += shift(lower_sum[i + 1], y=-k)
    pulled = jnp.concatenate([upper_grad, lower_grad])

    line = lax.all_to_all(
        jnp.broadcast_to(squares[None], (16, 8, 128)), ("zh", "zl", "core"), 0, 0
    )
    total = jnp.sum(line, axis=0)
    for axis in ("x", "y"):
        near = [shift(total, **{axis: k}) for k in (1, 2, 3)]
        total = (total + near[1]) + (near[0] + near[2])
    distance = total[0, 0] / jnp.float32(texts * 256)
    return distance, pulled


def solution(mesh):
    fine = Mesh(mesh.devices.reshape(SIZES), AXES)
    spec = P(AXES, None)
    return jax.shard_map(
        shards, mesh=fine, in_specs=(spec, spec), out_specs=(P(), spec), check_vma=False
    )
```

```python
import jax
import jax.numpy as jnp
from jax import lax
from jax.experimental import pallas as pl
from jax.experimental.pallas import tpu as pltpu
from jax.sharding import Mesh, PartitionSpec as P

AXES = ("y", "zl", "zh", "x", "core")
SIZES = (4, 4, 2, 4, 2)
DEPTH = 1024


def join_kernel(student_ref, teacher_ref, both_ref, upper_ref, lower_ref):
    width = student_ref.shape[1]
    half = upper_ref.shape[1]
    for source, place in ((student_ref, slice(0, width)), (teacher_ref, slice(width, None))):
        both_ref[:, place] = source[...]
        for i in range(4):
            upper_ref[i, :, place] = source[:half]
            lower_ref[i, :, place] = source[half:]


def join(student, teacher):
    texts, total = student.shape[0], student.shape[1] + teacher.shape[1]
    whole = jax.ShapeDtypeStruct((texts, total), student.dtype)
    part = jax.ShapeDtypeStruct((4, texts // 2, total), student.dtype)
    return pl.pallas_call(join_kernel, out_shape=(whole, part, part))(student, teacher)


def excess_kernel(
    upper_ref, lower_ref, rows_ref,
    upper_out, lower_out, squares_ref,
    cols, rows, total, rounded, sems,
):
    count, width = upper_ref.shape[0], upper_out.shape[1]
    steps = rows.shape[0]
    copies = []
    for k in range(steps):
        block = pl.ds(k * DEPTH, DEPTH)
        moves = (
            (upper_ref.at[:, block], cols.at[k, pl.ds(0, count)]),
            (lower_ref.at[:, block], cols.at[k, pl.ds(count, count)]),
            (rows_ref.at[:, block], rows.at[k]),
        )
        copies.append(
            [pltpu.make_async_copy(a, b, sems.at[k, i]) for i, (a, b) in enumerate(moves)]
        )
        for copy in copies[-1]:
            copy.start()
    for k in range(steps):
        for copy in copies[k]:
            copy.wait()
        product = lax.dot_general(
            cols[k], rows[k], (((1,), (1,)), ((), ())), preferred_element_type=jnp.float32
        )
        if k == 0:
            total[...] = product
        elif k * DEPTH < width:
            total[...] += product
        else:
            total[...] -= product
    excess = total[...]
    rounded[...] = excess.astype(rounded.dtype)
    squares = jnp.sum(jnp.sum(excess * excess, axis=0, keepdims=True), axis=1, keepdims=True)
    squares_ref[...] = jnp.broadcast_to(squares[None], squares_ref.shape)
    for k in range(width // DEPTH):
        place = slice(k * DEPTH, (k + 1) * DEPTH)
        for half, out in enumerate((upper_out, lower_out)):
            out[:, place] = jnp.dot(
                rounded[half * count : (half + 1) * count],
                rows[k],
                preferred_element_type=jnp.float32,
            )


def pulls(upper, lower, rows, student_width):
    texts, width = rows.shape
    count = upper.shape[0]
    anywhere = pl.BlockSpec(memory_space=pl.ANY)
    partial_term = jax.ShapeDtypeStruct((count, student_width), jnp.float32)
    return pl.pallas_call(
        excess_kernel,
        in_specs=[anywhere] * 3,
        out_shape=(
            partial_term, partial_term, jax.ShapeDtypeStruct((16, 8, 128), jnp.float32)
        ),
        scratch_shapes=[
            pltpu.VMEM((width // DEPTH, 2 * count, DEPTH), jnp.bfloat16),
            pltpu.VMEM((width // DEPTH, texts, DEPTH), jnp.bfloat16),
            pltpu.VMEM((2 * count, texts), jnp.float32),
            pltpu.VMEM((2 * count, texts), jnp.bfloat16),
            pltpu.SemaphoreType.DMA((width // DEPTH, 3)),
        ],
        compiler_params=pltpu.CompilerParams(vmem_limit_bytes=56 * 1024 * 1024),
        cost_estimate=pl.CostEstimate(
            flops=4 * count * texts * (width + student_width),
            bytes_accessed=2 * (2 * count + texts) * width + 8 * count * student_width,
            transcendentals=0,
        ),
    )(upper, lower, rows)


def swap(value, axes):
    return lax.all_to_all(value, axes, 0, 0)


def shards(student, teacher):
    texts, width = student.shape
    both, upper, lower = join(student, teacher)
    rows = lax.all_gather(both, ("zh", "zl", "core"), axis=0, tiled=True)
    to_all = lambda value: jnp.broadcast_to(value[None], (4,) + value.shape)
    upper, lower = swap(upper, "x"), swap(lower, "y")
    upper, lower = swap(to_all(upper), "y"), swap(to_all(lower), "x")
    flat = lambda value: value.reshape(-1, value.shape[-1])
    upper, lower, squares = pulls(flat(upper), flat(lower), rows, width)
    unflat = lambda value: value.reshape(4, 4, texts // 2, width)
    upper = jnp.sum(swap(unflat(upper), "y"), axis=0)
    lower = jnp.sum(swap(unflat(lower), "x"), axis=0)
    upper = jnp.sum(swap(upper, "x"), axis=0)
    lower = jnp.sum(swap(lower, "y"), axis=0)
    pulled = jnp.concatenate([upper, lower])

    line = jnp.sum(swap(squares, ("zh", "zl", "core")), axis=0)
    plane = swap(jnp.broadcast_to(line[None], (16, 8, 128)), ("y", "x"))
    distance = jnp.sum(plane[:, 0, 0]) / jnp.float32(texts * 256)
    return distance, pulled


def solution(mesh):
    fine = Mesh(mesh.devices.reshape(SIZES), AXES)
    spec = P(AXES, None)
    return jax.shard_map(
        shards, mesh=fine, in_specs=(spec, spec), out_specs=(P(), spec), check_vma=False
    )
```

```python
import jax
import jax.numpy as jnp
from jax import lax
from jax.experimental import pallas as pl
from jax.experimental.pallas import tpu as pltpu
from jax.sharding import Mesh, PartitionSpec as P

AXES = ("y", "zl", "zh", "x", "core")
SIZES = (4, 4, 2, 4, 2)
STRIDES = dict(zip(AXES, (64, 16, 8, 2, 1)))
NEAR = (2, 1, 3)
DEPTH = 1024


def shift(value, axes, step):
    pairs = []
    for target in range(256):
        stride = STRIDES[axes[target % 2]]
        place = target // stride % 4
        pairs.append((target + ((place + step) % 4 - place) * stride, target))
    return lax.ppermute(value, AXES, pairs)


def join_kernel(student_ref, teacher_ref, both_ref):
    width = student_ref.shape[1]
    both_ref[:, :width] = student_ref[...]
    both_ref[:, width:] = teacher_ref[...]


def join(student, teacher):
    texts, total = student.shape[0], student.shape[1] + teacher.shape[1]
    return pl.pallas_call(
        join_kernel, out_shape=jax.ShapeDtypeStruct((texts, total), student.dtype)
    )(student, teacher)


def excess_kernel(*refs):
    bundles, rows_ref, outs = refs[:4], refs[4], refs[5:9]
    squares_ref, rows, total, rounded, sems = refs[9:]
    count, width = outs[0].shape
    steps = rows.shape[0]
    copies = [
        pltpu.make_async_copy(rows_ref.at[:, pl.ds(k * DEPTH, DEPTH)], rows.at[k], sems.at[k])
        for k in range(steps)
    ]
    for copy in copies:
        copy.start()
    for k in range(steps):
        place = slice(k * DEPTH, (k + 1) * DEPTH)
        cols = jnp.concatenate([bundle[:, place] for bundle in bundles])
        copies[k].wait()
        product = lax.dot_general(
            cols, rows[k], (((1,), (1,)), ((), ())), preferred_element_type=jnp.float32
        )
        if k == 0:
            total[...] = product
        elif k * DEPTH < width:
            total[...] += product
        else:
            total[...] -= product
    excess = total[...]
    rounded[...] = excess.astype(rounded.dtype)
    squares = jnp.sum(jnp.sum(excess * excess, axis=0, keepdims=True), axis=1, keepdims=True)
    squares_ref[...] = jnp.broadcast_to(squares[None], squares_ref.shape)
    for k in range(width // DEPTH):
        place = slice(k * DEPTH, (k + 1) * DEPTH)
        product = jnp.dot(rounded[...], rows[k], preferred_element_type=jnp.float32)
        for i, out in enumerate(outs):
            out[:, place] = product[i * count : (i + 1) * count]


def pulls(bundles, rows, student_width):
    texts, width = rows.shape
    count = bundles[0].shape[0]
    inside = pl.BlockSpec(memory_space=pltpu.VMEM)
    partial_term = jax.ShapeDtypeStruct((count, student_width), jnp.float32)
    return pl.pallas_call(
        excess_kernel,
        in_specs=[inside] * 4 + [pl.BlockSpec(memory_space=pl.ANY)],
        out_specs=(inside,) * 5,
        out_shape=(partial_term,) * 4 + (jax.ShapeDtypeStruct((16, 8, 128), jnp.float32),),
        scratch_shapes=[
            pltpu.VMEM((width // DEPTH, texts, DEPTH), jnp.bfloat16),
            pltpu.VMEM((4 * count, texts), jnp.float32),
            pltpu.VMEM((4 * count, texts), jnp.bfloat16),
            pltpu.SemaphoreType.DMA((width // DEPTH,)),
        ],
        compiler_params=pltpu.CompilerParams(vmem_limit_bytes=40 * 1024 * 1024),
        cost_estimate=pl.CostEstimate(
            flops=8 * count * texts * (width + student_width),
            bytes_accessed=2 * texts * width,
            transcendentals=0,
        ),
    )(*bundles, rows)


def shards(student, teacher):
    texts, width = student.shape
    both = join(student, teacher)
    rows = lax.all_gather(both, ("zh", "zl", "core"), axis=0, tiled=True)
    near, far = ("x", "y"), ("y", "x")
    own = jnp.concatenate([both] + [shift(both, near, k) for k in NEAR])
    bundles = [own] + [shift(own, far, k) for k in NEAR]
    *terms, squares = pulls(bundles, rows, width)
    partial_term = terms[0]
    for i, k in enumerate(NEAR):
        back = shift(terms[i + 1], far, -k)
        if i == 0:
            back, squares = lax.optimization_barrier((back, squares))
        partial_term += back
    blocks = partial_term.reshape(4, texts, width)
    pulled = blocks[0]
    for i, k in enumerate(NEAR):
        pulled += shift(blocks[i + 1], near, -k)

    line = jnp.sum(
        lax.all_to_all(squares, ("zh", "zl", "core"), 0, 0), axis=0, keepdims=True
    )
    plane = lax.all_to_all(jnp.broadcast_to(line, (16, 8, 128)), ("y", "x"), 0, 0)
    distance = jnp.sum(plane[:, 0, 0]) / jnp.float32(texts * 256)
    return distance, pulled


def solution(mesh):
    fine = Mesh(mesh.devices.reshape(SIZES), AXES)
    spec = P(AXES, None)
    return jax.shard_map(
        shards, mesh=fine, in_specs=(spec, spec), out_specs=(P(), spec), check_vma=False
    )
```

```python
import jax
import jax.numpy as jnp
from jax import lax
from jax.experimental import pallas as pl
from jax.experimental.pallas import tpu as pltpu
from jax.sharding import Mesh, PartitionSpec as P

AXES = ("y", "zl", "zh", "x", "core")
SIZES = (4, 4, 2, 4, 2)
STRIDES = dict(zip(AXES, (64, 16, 8, 2, 1)))
DEPTH = 1024
EXTRA = 16


def shift(value, axes, step):
    pairs = []
    for target in range(256):
        stride = STRIDES[axes[target % 2]]
        place = target // stride % 4
        pairs.append((target + ((place + step) % 4 - place) * stride, target))
    return lax.ppermute(value, AXES, pairs)


def join_kernel(student_ref, teacher_ref, both_ref):
    width = student_ref.shape[1]
    both_ref[:, :width] = student_ref[...]
    both_ref[:, width:] = teacher_ref[...]


def join(student, teacher):
    texts, total = student.shape[0], student.shape[1] + teacher.shape[1]
    return pl.pallas_call(
        join_kernel, out_shape=jax.ShapeDtypeStruct((texts, total), student.dtype)
    )(student, teacher)


def excess_kernel(*refs):
    pieces, rows_ref, outs = refs[:8], refs[8], refs[9:12]
    own_ref, squares_ref, cols, rows, total, rounded, sems = refs[12:]
    height = pieces[0].shape[0]
    count = own_ref.shape[0]
    width = outs[0].shape[1]
    steps = rows.shape[0]
    copies = []
    for k in range(steps):
        block = pl.ds(k * DEPTH, DEPTH)
        moves = [(rows_ref.at[:, block], rows.at[k])]
        for i, piece in enumerate(pieces):
            moves.append((piece.at[:, block], cols.at[k, pl.ds(i * height, height)]))
        copies.append(
            [pltpu.make_async_copy(a, b, sems.at[k, i]) for i, (a, b) in enumerate(moves)]
        )
        for copy in copies[-1]:
            copy.start()
    for k in range(steps):
        for copy in copies[k]:
            copy.wait()
        product = lax.dot_general(
            cols[k], rows[k], (((1,), (1,)), ((), ())), preferred_element_type=jnp.float32
        )
        if k == 0:
            total[...] = product
        elif k * DEPTH < width:
            total[...] += product
        else:
            total[...] -= product
    excess = total[...]
    rounded[...] = excess.astype(rounded.dtype)
    squares = jnp.sum(jnp.sum(excess * excess, axis=0, keepdims=True), axis=1, keepdims=True)
    squares_ref[...] = jnp.broadcast_to(squares[None], squares_ref.shape)
    own_ref[...] = rounded[3 * count :]
    largest = [jnp.full((1, 1), 1e-36, jnp.float32)] * 3
    for k in range(width // DEPTH):
        place = slice(k * DEPTH, (k + 1) * DEPTH)
        product = jnp.dot(rounded[: 3 * count], rows[k], preferred_element_type=jnp.float32)
        for i, out in enumerate(outs):
            part = product[i * count : (i + 1) * count]
            out[:count, place] = part
            most = jnp.max(jnp.max(jnp.abs(part), axis=0, keepdims=True), axis=1, keepdims=True)
            largest[i] = jnp.maximum(largest[i], most)
    for most, out in zip(largest, outs):
        power = jnp.minimum(jnp.floor(14.0 - jnp.log2(most)), 120.0)
        out[:count] = out[:count] * jnp.exp2(power)
        out[count:] = jnp.broadcast_to(power, (EXTRA, width))


def pulls(pieces, rows, student_width):
    texts, width = rows.shape
    count = 2 * pieces[0].shape[0]
    inside = pl.BlockSpec(memory_space=pltpu.VMEM)
    scaled = jax.ShapeDtypeStruct((count + EXTRA, student_width), jnp.float32)
    return pl.pallas_call(
        excess_kernel,
        in_specs=[pl.BlockSpec(memory_space=pltpu.HBM)] * 9,
        out_specs=(inside,) * 5,
        out_shape=(scaled,) * 3
        + (
            jax.ShapeDtypeStruct((count, texts), jnp.bfloat16),
            jax.ShapeDtypeStruct((16, 8, 128), jnp.float32),
        ),
        scratch_shapes=[
            pltpu.VMEM((width // DEPTH, 4 * count, DEPTH), jnp.bfloat16),
            pltpu.VMEM((width // DEPTH, texts, DEPTH), jnp.bfloat16),
            pltpu.VMEM((4 * count, texts), jnp.float32),
            pltpu.VMEM((4 * count, texts), jnp.bfloat16),
            pltpu.SemaphoreType.DMA((width // DEPTH, 9)),
        ],
        compiler_params=pltpu.CompilerParams(vmem_limit_bytes=VMEM_LIMIT),
        cost_estimate=pl.CostEstimate(
            flops=8 * count * texts * (width + student_width),
            bytes_accessed=2 * (4 * count + texts) * width,
            transcendentals=0,
        ),
    )(*pieces, rows)


VMEM_LIMIT = 56 * 1024 * 1024


def shards(student, teacher):
    texts, width = student.shape
    both = join(student, teacher)
    rows = lax.all_gather(both, ("zh", "zl", "core"), axis=0, tiled=True)
    near, far = ("x", "y"), ("y", "x")
    first = jnp.concatenate([both, shift(both, near, 1)])
    second = jnp.concatenate([shift(both, near, 3), shift(both, near, 2)])
    first_up, first_down = shift(first, far, 1), shift(first, far, 3)
    second_down, second_up = shift(second, far, 3), shift(second, far, 1)
    pieces = (shift(first_up, far, 1), shift(second_down, far, 3))
    pieces += (first_up, second_up, first_down, second_down, first, second)
    *scaled, own, squares = pulls(pieces, rows, width)
    *sent, own, squares = lax.optimization_barrier(
        [term.astype(jnp.float16) for term in scaled] + [own, squares]
    )
    returned = [shift(term, far, -k) for term, k in zip(sent, (2, 1, 3))]
    returned[1], squares = lax.optimization_barrier((returned[1], squares))
    partial_term = jnp.dot(own, rows[:, :width], preferred_element_type=jnp.float32)
    count = own.shape[0]
    for term in returned:
        scale = jnp.exp2(-term[count : count + 1].astype(jnp.float32))
        partial_term += term[:count].astype(jnp.float32) * scale
    blocks = partial_term.reshape(4, texts, width)
    pulled = blocks[0]
    for i, k in ((3, 2), (1, 1), (2, 3)):
        pulled += shift(blocks[i], near, -k)

    line = jnp.sum(
        lax.all_to_all(squares, ("zh", "zl", "core"), 0, 0), axis=0, keepdims=True
    )
    plane = lax.all_to_all(jnp.broadcast_to(line, (16, 8, 128)), ("y", "x"), 0, 0)
    distance = jnp.sum(plane[:, 0, 0]) / jnp.float32(texts * 256)
    return distance, pulled


def solution(mesh):
    fine = Mesh(mesh.devices.reshape(SIZES), AXES)
    spec = P(AXES, None)
    return jax.shard_map(
        shards, mesh=fine, in_specs=(spec, spec), out_specs=(P(), spec), check_vma=False
    )
```

```python
import jax
import jax.numpy as jnp
from jax import lax
from jax.experimental import pallas as pl
from jax.experimental.pallas import tpu as pltpu
from jax.sharding import Mesh, PartitionSpec as P

AXES = ("y", "zl", "zh", "x", "core")
SIZES = (4, 4, 2, 4, 2)
STRIDES = dict(zip(AXES, (64, 16, 8, 2, 1)))
DEPTH = 1024
EXTRA = 16


def shift(value, axes, step):
    pairs = []
    for target in range(256):
        stride = STRIDES[axes[target % 2]]
        place = target // stride % 4
        pairs.append((target + ((place + step) % 4 - place) * stride, target))
    return lax.ppermute(value, AXES, pairs)


def round_z(value):
    pairs = []
    for target in range(256):
        z = target // 16 % 4 + target // 8 % 2 * 4
        source = (z - 1 + target % 2 * 2) % 8
        pairs.append((target + (source % 4 - z % 4) * 16 + (source // 4 - z // 4) * 8, target))
    return lax.ppermute(value, AXES, pairs)


def other_core(value):
    return lax.ppermute(value, "core", [(0, 1), (1, 0)])


def join_kernel(student_ref, teacher_ref, both_ref):
    width = student_ref.shape[1]
    both_ref[:, :width] = student_ref[...]
    both_ref[:, width:] = teacher_ref[...]


def join(student, teacher):
    texts, total = student.shape[0], student.shape[1] + teacher.shape[1]
    return pl.pallas_call(
        join_kernel, out_shape=jax.ShapeDtypeStruct((texts, total), student.dtype)
    )(student, teacher)


def excess_kernel(*refs):
    pieces, lines, outs = refs[:8], refs[8:17], refs[17:20]
    own_ref, squares_ref, rows, total, rounded = refs[20:]
    count = own_ref.shape[0]
    width = outs[0].shape[1]
    for k in range(pieces[0].shape[1] // DEPTH):
        place = slice(k * DEPTH, (k + 1) * DEPTH)
        cols = jnp.concatenate([piece[:, place] for piece in pieces])
        line = jnp.concatenate([piece[:, place] for piece in lines])
        product = lax.dot_general(
            cols, line, (((1,), (1,)), ((), ())), preferred_element_type=jnp.float32
        )
        if k * DEPTH < width:
            rows[k] = line
        if k == 0:
            total[...] = product
        elif k * DEPTH < width:
            total[...] += product
        else:
            total[...] -= product
    excess = total[...]
    rounded[...] = excess.astype(rounded.dtype)
    squares = jnp.sum(jnp.sum(excess * excess, axis=0, keepdims=True), axis=1, keepdims=True)
    squares_ref[...] = jnp.broadcast_to(squares, squares_ref.shape)
    own_ref[...] = rounded[3 * count :]
    largest = [jnp.full((1, 1), 1e-36, jnp.float32)] * 3
    for k in range(width // DEPTH):
        place = slice(k * DEPTH, (k + 1) * DEPTH)
        product = jnp.dot(rounded[: 3 * count], rows[k], preferred_element_type=jnp.float32)
        for i, out in enumerate(outs):
            part = product[i * count : (i + 1) * count]
            out[:count, place] = part
            most = jnp.max(jnp.max(jnp.abs(part), axis=0, keepdims=True), axis=1, keepdims=True)
            largest[i] = jnp.maximum(largest[i], most)
    for most, out in zip(largest, outs):
        power = jnp.minimum(jnp.floor(14.0 - jnp.log2(most)), 120.0)
        out[:count] = out[:count] * jnp.exp2(power)
        out[count:] = jnp.broadcast_to(power, (EXTRA, width))


def own_kernel(own_ref, squares_ref, *refs):
    lines, out_ref, spread_ref = refs[:9], refs[9], refs[10]
    line = jnp.concatenate([piece[...] for piece in lines])
    out_ref[...] = jnp.dot(own_ref[...], line, preferred_element_type=jnp.float32)
    spread_ref[...] = jnp.broadcast_to(squares_ref[...][None], spread_ref.shape)


def pulls(pieces, lines, student_width):
    width = lines[0].shape[1]
    texts = sum(line.shape[0] for line in lines)
    count = 2 * pieces[0].shape[0]
    inside = pl.BlockSpec(memory_space=pltpu.VMEM)
    scaled = jax.ShapeDtypeStruct((count + EXTRA, student_width), jnp.float32)
    return pl.pallas_call(
        excess_kernel,
        in_specs=[inside] * 17,
        out_specs=(inside,) * 5,
        out_shape=(scaled,) * 3
        + (
            jax.ShapeDtypeStruct((count, texts), jnp.bfloat16),
            jax.ShapeDtypeStruct((8, 128), jnp.float32),
        ),
        scratch_shapes=[
            pltpu.VMEM((student_width // DEPTH, texts, DEPTH), jnp.bfloat16),
            pltpu.VMEM((4 * count, texts), jnp.float32),
            pltpu.VMEM((4 * count, texts), jnp.bfloat16),
        ],
        compiler_params=pltpu.CompilerParams(vmem_limit_bytes=VMEM_LIMIT),
        cost_estimate=pl.CostEstimate(
            flops=8 * count * texts * (width + student_width),
            bytes_accessed=2 * (4 * count + texts) * width,
            transcendentals=0,
        ),
    )(*pieces, *lines)


def own_pull(own, squares, lines, student_width):
    count, texts = own.shape
    whole = lambda shape: pl.BlockSpec(shape, lambda i: (0,) * len(shape))
    return pl.pallas_call(
        own_kernel,
        grid=(1,),
        in_specs=[whole(own.shape), whole(squares.shape)]
        + [whole((line.shape[0], student_width)) for line in lines],
        out_specs=(whole((count, student_width)), whole((64,) + squares.shape)),
        out_shape=(
            jax.ShapeDtypeStruct((count, student_width), jnp.float32),
            jax.ShapeDtypeStruct((64,) + squares.shape, jnp.float32),
        ),
        compiler_params=pltpu.CompilerParams(vmem_limit_bytes=VMEM_LIMIT),
        cost_estimate=pl.CostEstimate(
            flops=2 * count * texts * student_width,
            bytes_accessed=2 * texts * student_width,
            transcendentals=0,
        ),
    )(own, squares, *lines)


VMEM_LIMIT = 24 * 1024 * 1024


def shards(student, teacher):
    texts, width = student.shape
    both = join(student, teacher)
    pair = jnp.concatenate([both, other_core(both)])
    lines = [pair]
    for step in range(4):
        arrived = round_z(lines[max(2 * step - 1, 0)][: pair.shape[0] if step < 3 else texts])
        lines += [arrived, other_core(arrived)]
    near, far = ("x", "y"), ("y", "x")
    first = jnp.concatenate([both, shift(both, near, 1)])
    second = jnp.concatenate([shift(both, near, 3), shift(both, near, 2)])
    first_up, first_down = shift(first, far, 1), shift(first, far, 3)
    second_down, second_up = shift(second, far, 3), shift(second, far, 1)
    pieces = (shift(first_up, far, 1), shift(second_down, far, 3))
    pieces += (first_up, second_up, first_down, second_down, first, second)
    *scaled, own, squares = pulls(pieces, lines, width)
    sent = [term.astype(jnp.float16) for term in scaled]
    returned = [shift(term, far, -k) for term, k in zip(sent, (2, 1, 3))]
    own, squares = lax.optimization_barrier((own, squares, *sent))[:2]
    partial_term, squares = own_pull(own, squares, lines, width)
    count = own.shape[0]
    for term in returned:
        scale = jnp.exp2(-term[count : count + 1].astype(jnp.float32))
        partial_term += term[:count].astype(jnp.float32) * scale
    blocks = partial_term.reshape(4, texts, width)
    pulled = blocks[0]
    for i, k in ((3, 2), (1, 1), (2, 3)):
        pulled += shift(blocks[i], near, -k)

    total = jnp.sum(lax.all_to_all(squares, ("y", "zh", "zl", "core"), 0, 0), axis=0)
    ring = [shift(total, ("x", "x"), k) for k in (1, 2, 3)]
    total = (total + ring[1]) + (ring[0] + ring[2])
    return total[0, 0] / jnp.float32(texts * 256), pulled


def solution(mesh):
    fine = Mesh(mesh.devices.reshape(SIZES), AXES)
    spec = P(AXES, None)
    return jax.shard_map(
        shards, mesh=fine, in_specs=(spec, spec), out_specs=(P(), spec), check_vma=False
    )
```

```python
import jax
import jax.numpy as jnp
from jax import lax
from jax.experimental import pallas as pl
from jax.experimental.pallas import tpu as pltpu
from jax.sharding import Mesh, PartitionSpec as P

AXES = ("y", "zl", "zh", "x", "core")
SIZES = (4, 4, 2, 4, 2)
STRIDES = dict(zip(AXES, (64, 16, 8, 2, 1)))
DEPTH = 1024
EXTRA = 16


def shift(value, axes, step):
    pairs = []
    for target in range(256):
        stride = STRIDES[axes[target % 2]]
        place = target // stride % 4
        pairs.append((target + ((place + step) % 4 - place) * stride, target))
    return lax.ppermute(value, AXES, pairs)


def round_z(value):
    pairs = []
    for target in range(256):
        z = target // 16 % 4 + target // 8 % 2 * 4
        source = (z - 1 + target % 2 * 2) % 8
        pairs.append((target + (source % 4 - z % 4) * 16 + (source // 4 - z // 4) * 8, target))
    return lax.ppermute(value, AXES, pairs)


def other_core(value):
    return lax.ppermute(value, "core", [(0, 1), (1, 0)])


def join_kernel(student_ref, teacher_ref, both_ref):
    width = student_ref.shape[1]
    both_ref[:, :width] = student_ref[...]
    both_ref[:, width:] = teacher_ref[...]


def join(student, teacher):
    texts, total = student.shape[0], student.shape[1] + teacher.shape[1]
    return pl.pallas_call(
        join_kernel, out_shape=jax.ShapeDtypeStruct((texts, total), student.dtype)
    )(student, teacher)


def excess_kernel(*refs):
    pieces, lines, outs = refs[:8], refs[8:-8], refs[-8:-5]
    own_ref, squares_ref, rows, total, rounded = refs[-5:]
    count = own_ref.shape[0]
    width = outs[0].shape[1]
    for k in range(pieces[0].shape[1] // DEPTH):
        place = slice(k * DEPTH, (k + 1) * DEPTH)
        cols = jnp.concatenate([piece[:, place] for piece in pieces])
        line = jnp.concatenate([piece[:, place] for piece in lines])
        product = lax.dot_general(
            cols, line, (((1,), (1,)), ((), ())), preferred_element_type=jnp.float32
        )
        if k * DEPTH < width:
            rows[k] = line
        if k == 0:
            total[...] = product
        elif k * DEPTH < width:
            total[...] += product
        else:
            total[...] -= product
    excess = total[...]
    rounded[...] = excess.astype(rounded.dtype)
    squares = jnp.sum(jnp.sum(excess * excess, axis=0, keepdims=True), axis=1, keepdims=True)
    squares_ref[...] = jnp.broadcast_to(squares, squares_ref.shape)
    own_ref[...] = rounded[3 * count :]
    largest = [jnp.full((1, 1), 1e-36, jnp.float32)] * 3
    for k in range(width // DEPTH):
        place = slice(k * DEPTH, (k + 1) * DEPTH)
        product = jnp.dot(rounded[: 3 * count], rows[k], preferred_element_type=jnp.float32)
        for i, out in enumerate(outs):
            part = product[i * count : (i + 1) * count]
            out[:count, place] = part
            most = jnp.max(jnp.max(jnp.abs(part), axis=0, keepdims=True), axis=1, keepdims=True)
            largest[i] = jnp.maximum(largest[i], most)
    for most, out in zip(largest, outs):
        power = jnp.clip(jnp.floor((14.0 - jnp.log2(most)) / 6.0), 0.0, 14.0)
        out[:count] = out[:count] * jnp.exp2(6.0 * power)
        out[count:] = jnp.broadcast_to(jnp.exp2(-power), (EXTRA, width))


def own_kernel(own_ref, squares_ref, *refs):
    *lines, out_ref, spread_ref = refs
    line = jnp.concatenate([piece[...] for piece in lines])
    out_ref[...] = jnp.dot(own_ref[...], line, preferred_element_type=jnp.float32)
    spread_ref[...] = jnp.broadcast_to(squares_ref[...][None], spread_ref.shape)


def pulls(pieces, lines, student_width):
    width = lines[0].shape[1]
    texts = sum(line.shape[0] for line in lines)
    count = 2 * pieces[0].shape[0]
    inside = pl.BlockSpec(memory_space=pltpu.VMEM)
    scaled = jax.ShapeDtypeStruct((count + EXTRA, student_width), jnp.float32)
    return pl.pallas_call(
        excess_kernel,
        in_specs=[inside] * (len(pieces) + len(lines)),
        out_specs=(inside,) * 5,
        out_shape=(scaled,) * 3
        + (
            jax.ShapeDtypeStruct((count, texts), jnp.bfloat16),
            jax.ShapeDtypeStruct((8, 128), jnp.float32),
        ),
        scratch_shapes=[
            pltpu.VMEM((student_width // DEPTH, texts, DEPTH), jnp.bfloat16),
            pltpu.VMEM((4 * count, texts), jnp.float32),
            pltpu.VMEM((4 * count, texts), jnp.bfloat16),
        ],
        compiler_params=pltpu.CompilerParams(vmem_limit_bytes=VMEM_LIMIT),
        cost_estimate=pl.CostEstimate(
            flops=8 * count * texts * (width + student_width),
            bytes_accessed=2 * (4 * count + texts) * width,
            transcendentals=0,
        ),
    )(*pieces, *lines)


def own_pull(own, squares, lines, student_width):
    count, texts = own.shape
    whole = lambda shape: pl.BlockSpec(shape, lambda i: (0,) * len(shape))
    return pl.pallas_call(
        own_kernel,
        grid=(1,),
        in_specs=[whole(own.shape), whole(squares.shape)]
        + [whole((line.shape[0], student_width)) for line in lines],
        out_specs=(whole((count, student_width)), whole((64,) + squares.shape)),
        out_shape=(
            jax.ShapeDtypeStruct((count, student_width), jnp.float32),
            jax.ShapeDtypeStruct((64,) + squares.shape, jnp.float32),
        ),
        compiler_params=pltpu.CompilerParams(vmem_limit_bytes=VMEM_LIMIT),
        cost_estimate=pl.CostEstimate(
            flops=2 * count * texts * student_width,
            bytes_accessed=2 * texts * student_width,
            transcendentals=0,
        ),
    )(own, squares, *lines)


VMEM_LIMIT = 24 * 1024 * 1024


def shards(student, teacher):
    texts, width = student.shape
    both = join(student, teacher)
    tie = lax.optimization_barrier
    near, far = ("x", "y"), ("y", "x")
    other = other_core(both)
    ring = [round_z(both)]
    both, other = tie((both, other))
    ring.append(round_z(other))
    right, left, across = (shift(both, near, k) for k in (1, 3, 2))
    lines = [both, other]
    ring = jnp.concatenate(ring)
    lines += [ring, other_core(ring)]
    ring, right, left, across = round_z(ring), *tie((right, left, across, ring))[:3]
    first, second = jnp.concatenate([both, right]), jnp.concatenate([left, across])
    first_up, second_down = shift(first, far, 1), shift(second, far, 3)
    ring, first, second = tie((ring, first, second))
    lines += [ring, other_core(ring)]
    ring = round_z(ring)
    first, second, first_up, second_down = tie((first, second, first_up, second_down))
    first_across, second_across = shift(first_up, far, 1), shift(second_down, far, 3)
    first_down, second_up = shift(first, far, 3), shift(second, far, 1)
    ring, first_up, second_down = tie((ring, first_up, second_down))
    lines += [ring, other_core(ring)]
    ring = round_z(ring[:texts])
    lines += [ring, other_core(ring)]
    pieces = (first_across, second_across)
    pieces += (first_up, second_up, first_down, second_down, first, second)
    *scaled, own, squares = pulls(pieces, lines, width)
    sent = [term.astype(jnp.float16) for term in scaled]
    returned = [shift(term, far, -k) for term, k in zip(sent, (2, 1, 3))]
    own, squares = lax.optimization_barrier((own, squares, *sent))[:2]
    partial_term, squares = own_pull(own, squares, lines, width)
    count = own.shape[0]
    for term in returned:
        root = term[count : count + 1].astype(jnp.float32)
        root = root * root * root
        partial_term += term[:count].astype(jnp.float32) * (root * root)
    blocks = partial_term.reshape(4, texts, width)
    pulled = blocks[0]
    for i, k in ((3, 2), (1, 1), (2, 3)):
        pulled += shift(blocks[i], near, -k)

    total = jnp.sum(lax.all_to_all(squares, ("y", "zh", "zl", "core"), 0, 0), axis=0)
    ring = [shift(total, ("x", "x"), k) for k in (1, 2, 3)]
    total = (total + ring[1]) + (ring[0] + ring[2])
    return total[0, 0] / jnp.float32(texts * 256), pulled


def solution(mesh):
    fine = Mesh(mesh.devices.reshape(SIZES), AXES)
    spec = P(AXES, None)
    return jax.shard_map(
        shards, mesh=fine, in_specs=(spec, spec), out_specs=(P(), spec), check_vma=False
    )
```

```python
import jax
import jax.numpy as jnp
from jax import lax
from jax.experimental import pallas as pl
from jax.experimental.pallas import tpu as pltpu
from jax.sharding import Mesh, PartitionSpec as P

AXES = ("y", "zl", "zh", "x", "core")
SIZES = (4, 4, 2, 4, 2)
STRIDES = dict(zip(AXES, (64, 16, 8, 2, 1)))
DEPTH = 1024
EXTRA = 16


def shift(value, axes, step):
    pairs = []
    for target in range(256):
        stride = STRIDES[axes[target % 2]]
        place = target // stride % 4
        pairs.append((target + ((place + step) % 4 - place) * stride, target))
    return lax.ppermute(value, AXES, pairs)


def round_z(value):
    pairs = []
    for target in range(256):
        z = target // 16 % 4 + target // 8 % 2 * 4
        source = (z - 1 + target % 2 * 2) % 8
        pairs.append((target + (source % 4 - z % 4) * 16 + (source // 4 - z // 4) * 8, target))
    return lax.ppermute(value, AXES, pairs)


def other_core(value):
    return lax.ppermute(value, "core", [(0, 1), (1, 0)])


def join_kernel(student_ref, teacher_ref, both_ref):
    width = student_ref.shape[1]
    both_ref[:, :width] = student_ref[...]
    both_ref[:, width:] = teacher_ref[...]


def join(student, teacher):
    texts, total = student.shape[0], student.shape[1] + teacher.shape[1]
    return pl.pallas_call(
        join_kernel, out_shape=jax.ShapeDtypeStruct((texts, total), student.dtype)
    )(student, teacher)


def excess_kernel(*refs):
    pieces, lines, outs = refs[:8], refs[8:-8], refs[-8:-5]
    own_ref, squares_ref, rows, total, rounded = refs[-5:]
    count = own_ref.shape[0]
    width = outs[0].shape[1]
    for k in range(pieces[0].shape[1] // DEPTH):
        place = slice(k * DEPTH, (k + 1) * DEPTH)
        cols = jnp.concatenate([piece[:, place] for piece in pieces])
        line = jnp.concatenate([piece[:, place] for piece in lines])
        product = lax.dot_general(
            cols, line, (((1,), (1,)), ((), ())), preferred_element_type=jnp.float32
        )
        if k * DEPTH < width:
            rows[k] = line
        if k == 0:
            total[...] = product
        elif k * DEPTH < width:
            total[...] += product
        else:
            total[...] -= product
    excess = total[...]
    rounded[...] = excess.astype(rounded.dtype)
    squares = jnp.sum(jnp.sum(excess * excess, axis=0, keepdims=True), axis=1, keepdims=True)
    squares_ref[...] = jnp.broadcast_to(squares, squares_ref.shape)
    own_ref[...] = rounded[3 * count :]
    largest = [jnp.full((1, 1), 1e-36, jnp.float32)] * 3
    for k in range(width // DEPTH):
        place = slice(k * DEPTH, (k + 1) * DEPTH)
        product = jnp.dot(rounded[: 3 * count], rows[k], preferred_element_type=jnp.float32)
        for i, out in enumerate(outs):
            part = product[i * count : (i + 1) * count]
            out[:count, place] = part
            most = jnp.max(jnp.max(jnp.abs(part), axis=0, keepdims=True), axis=1, keepdims=True)
            largest[i] = jnp.maximum(largest[i], most)
    for most, out in zip(largest, outs):
        power = jnp.clip(jnp.floor((14.0 - jnp.log2(most)) / 6.0), 0.0, 14.0)
        out[:count] = out[:count] * jnp.exp2(6.0 * power)
        out[count:] = jnp.broadcast_to(jnp.exp2(-power), (EXTRA, width))


def own_kernel(own_ref, squares_ref, *refs):
    *lines, out_ref, spread_ref = refs
    line = jnp.concatenate([piece[...] for piece in lines])
    out_ref[...] = jnp.dot(own_ref[...], line, preferred_element_type=jnp.float32)
    spread_ref[...] = jnp.broadcast_to(squares_ref[...][None], spread_ref.shape)


def pulls(pieces, lines, student_width):
    width = lines[0].shape[1]
    texts = sum(line.shape[0] for line in lines)
    count = 2 * pieces[0].shape[0]
    inside = pl.BlockSpec(memory_space=pltpu.VMEM)
    scaled = jax.ShapeDtypeStruct((count + EXTRA, student_width), jnp.float32)
    return pl.pallas_call(
        excess_kernel,
        in_specs=[inside] * (len(pieces) + len(lines)),
        out_specs=(inside,) * 5,
        out_shape=(scaled,) * 3
        + (
            jax.ShapeDtypeStruct((count, texts), jnp.bfloat16),
            jax.ShapeDtypeStruct((1, 128), jnp.float32),
        ),
        scratch_shapes=[
            pltpu.VMEM((student_width // DEPTH, texts, DEPTH), jnp.bfloat16),
            pltpu.VMEM((4 * count, texts), jnp.float32),
            pltpu.VMEM((4 * count, texts), jnp.bfloat16),
        ],
        compiler_params=pltpu.CompilerParams(vmem_limit_bytes=VMEM_LIMIT),
        cost_estimate=pl.CostEstimate(
            flops=8 * count * texts * (width + student_width),
            bytes_accessed=2 * (4 * count + texts) * width,
            transcendentals=0,
        ),
    )(*pieces, *lines)


def own_pull(own, squares, lines, student_width):
    count, texts = own.shape
    whole = lambda shape: pl.BlockSpec(shape, lambda i: (0,) * len(shape))
    return pl.pallas_call(
        own_kernel,
        grid=(1,),
        in_specs=[whole(own.shape), whole(squares.shape)]
        + [whole((line.shape[0], student_width)) for line in lines],
        out_specs=(whole((count, student_width)), whole((64,) + squares.shape)),
        out_shape=(
            jax.ShapeDtypeStruct((count, student_width), jnp.float32),
            jax.ShapeDtypeStruct((64,) + squares.shape, jnp.float32),
        ),
        compiler_params=pltpu.CompilerParams(vmem_limit_bytes=VMEM_LIMIT),
        cost_estimate=pl.CostEstimate(
            flops=2 * count * texts * student_width,
            bytes_accessed=2 * texts * student_width,
            transcendentals=0,
        ),
    )(own, squares, *lines)


VMEM_LIMIT = 24 * 1024 * 1024


def shards(student, teacher):
    texts, width = student.shape
    both = join(student, teacher)
    tie = lax.optimization_barrier
    near, far = ("x", "y"), ("y", "x")
    other = other_core(both)
    ring = [round_z(both)]
    both, other = tie((both, other))
    ring.append(round_z(other))
    right, left, across = (shift(both, near, k) for k in (1, 3, 2))
    lines = [both, other]
    ring = jnp.concatenate(ring)
    lines += [ring, other_core(ring)]
    ring, right, left, across = round_z(ring), *tie((right, left, across, ring))[:3]
    first, second = jnp.concatenate([both, right]), jnp.concatenate([left, across])
    first_up, second_down = shift(first, far, 1), shift(second, far, 3)
    ring, first, second = tie((ring, first, second))
    lines += [ring, other_core(ring)]
    ring = round_z(ring)
    first, second, first_up, second_down = tie((first, second, first_up, second_down))
    first_across, second_across = shift(first_up, far, 1), shift(second_down, far, 3)
    first_down, second_up = shift(first, far, 3), shift(second, far, 1)
    ring, first_up, second_down = tie((ring, first_up, second_down))
    lines += [ring, other_core(ring)]
    ring = round_z(ring[:texts])
    lines += [ring, other_core(ring)]
    pieces = (first_across, second_across)
    pieces += (first_up, second_up, first_down, second_down, first, second)
    *scaled, own, squares = pulls(pieces, lines, width)
    sent = [term.astype(jnp.float16) for term in scaled]
    returned = [shift(term, far, -k) for term, k in zip(sent, (2, 1, 3))]
    own, squares = lax.optimization_barrier((own, squares, *sent))[:2]
    partial_term, squares = own_pull(own, squares, lines, width)
    count = own.shape[0]
    for term in returned:
        root = term[count : count + 1].astype(jnp.float32)
        root = root * root * root
        partial_term += term[:count].astype(jnp.float32) * (root * root)
    blocks = partial_term.reshape(4, texts, width)
    pulled = blocks[0]
    for i, k in ((3, 2), (1, 1), (2, 3)):
        pulled += shift(blocks[i], near, -k)

    total = jnp.sum(lax.all_to_all(squares, ("y", "zh", "zl", "core"), 0, 0), axis=0)
    ring = [shift(total, ("x", "x"), k) for k in (1, 2, 3)]
    total = (total + ring[1]) + (ring[0] + ring[2])
    return total[0, 0] / jnp.float32(texts * 256), pulled


def solution(mesh):
    fine = Mesh(mesh.devices.reshape(SIZES), AXES)
    spec = P(AXES, None)
    return jax.shard_map(
        shards, mesh=fine, in_specs=(spec, spec), out_specs=(P(), spec), check_vma=False
    )
```

```python
import jax
import jax.numpy as jnp
from jax import lax
from jax.experimental import pallas as pl
from jax.experimental.pallas import tpu as pltpu
from jax.sharding import Mesh, PartitionSpec as P

AXES = ("y", "zl", "zh", "x", "core")
SIZES = (4, 4, 2, 4, 2)
STRIDES = dict(zip(AXES, (64, 16, 8, 2, 1)))
DEPTH = 1024
EXTRA = 16


def shift(value, axes, step):
    pairs = []
    for target in range(256):
        stride = STRIDES[axes[target % 2]]
        place = target // stride % 4
        pairs.append((target + ((place + step) % 4 - place) * stride, target))
    return lax.ppermute(value, AXES, pairs)


def round_z(value):
    pairs = []
    for target in range(256):
        z = target // 16 % 4 + target // 8 % 2 * 4
        source = (z - 1 + target % 2 * 2) % 8
        pairs.append((target + (source % 4 - z % 4) * 16 + (source // 4 - z // 4) * 8, target))
    return lax.ppermute(value, AXES, pairs)


def other_core(value):
    return lax.ppermute(value, "core", [(0, 1), (1, 0)])


def join_kernel(student_ref, teacher_ref, both_ref):
    width = student_ref.shape[1]
    both_ref[:, :width] = student_ref[...]
    both_ref[:, width:] = teacher_ref[...]


def join(student, teacher):
    texts, total = student.shape[0], student.shape[1] + teacher.shape[1]
    return pl.pallas_call(
        join_kernel, out_shape=jax.ShapeDtypeStruct((texts, total), student.dtype)
    )(student, teacher)


def excess_kernel(*refs):
    pieces, lines, outs = refs[:8], refs[8:-8], refs[-8:-5]
    own_ref, squares_ref, rows, total, rounded = refs[-5:]
    count = own_ref.shape[0]
    width = outs[0].shape[1]
    for k in range(pieces[0].shape[1] // DEPTH):
        place = slice(k * DEPTH, (k + 1) * DEPTH)
        cols = jnp.concatenate([piece[:, place] for piece in pieces])
        line = jnp.concatenate([piece[:, place] for piece in lines])
        product = lax.dot_general(
            cols, line, (((1,), (1,)), ((), ())), preferred_element_type=jnp.float32
        )
        if k * DEPTH < width:
            rows[k] = line
        if k == 0:
            total[...] = product
        elif k * DEPTH < width:
            total[...] += product
        else:
            total[...] -= product
    excess = total[...]
    rounded[...] = excess.astype(rounded.dtype)
    squares = jnp.sum(jnp.sum(excess * excess, axis=0, keepdims=True), axis=1, keepdims=True)
    squares_ref[...] = jnp.broadcast_to(squares, squares_ref.shape)
    own_ref[...] = rounded[3 * count :]
    largest = [jnp.full((1, 1), 1e-36, jnp.float32)] * 3
    for k in range(width // DEPTH):
        place = slice(k * DEPTH, (k + 1) * DEPTH)
        product = jnp.dot(rounded[: 3 * count], rows[k], preferred_element_type=jnp.float32)
        for i, out in enumerate(outs):
            part = product[i * count : (i + 1) * count]
            out[:count, place] = part
            most = jnp.max(jnp.max(jnp.abs(part), axis=0, keepdims=True), axis=1, keepdims=True)
            largest[i] = jnp.maximum(largest[i], most)
    for most, out in zip(largest, outs):
        power = jnp.clip(jnp.floor((14.0 - jnp.log2(most)) / 6.0), 0.0, 14.0)
        out[:count] = out[:count] * jnp.exp2(6.0 * power)
        out[count:] = jnp.broadcast_to(jnp.exp2(-power), (EXTRA, width))


def own_kernel(own_ref, squares_ref, *refs):
    *lines, out_ref, spread_ref = refs
    line = jnp.concatenate([piece[...] for piece in lines])
    out_ref[...] = jnp.dot(own_ref[...], line, preferred_element_type=jnp.float32)
    spread_ref[...] = jnp.broadcast_to(squares_ref[...][None], spread_ref.shape)


def pulls(pieces, lines, student_width):
    width = lines[0].shape[1]
    texts = sum(line.shape[0] for line in lines)
    count = 2 * pieces[0].shape[0]
    inside = pl.BlockSpec(memory_space=pltpu.VMEM)
    scaled = jax.ShapeDtypeStruct((count + EXTRA, student_width), jnp.float32)
    return pl.pallas_call(
        excess_kernel,
        in_specs=[inside] * (len(pieces) + len(lines)),
        out_specs=(inside,) * 5,
        out_shape=(scaled,) * 3
        + (
            jax.ShapeDtypeStruct((count, texts), jnp.bfloat16),
            jax.ShapeDtypeStruct((1, 128), jnp.float32),
        ),
        scratch_shapes=[
            pltpu.VMEM((student_width // DEPTH, texts, DEPTH), jnp.bfloat16),
            pltpu.VMEM((4 * count, texts), jnp.float32),
            pltpu.VMEM((4 * count, texts), jnp.bfloat16),
        ],
        compiler_params=pltpu.CompilerParams(vmem_limit_bytes=VMEM_LIMIT),
        cost_estimate=pl.CostEstimate(
            flops=8 * count * texts * (width + student_width),
            bytes_accessed=2 * (4 * count + texts) * width,
            transcendentals=0,
        ),
    )(*pieces, *lines)


def own_pull(own, squares, lines, student_width):
    count, texts = own.shape
    whole = lambda shape: pl.BlockSpec(shape, lambda i: (0,) * len(shape))
    return pl.pallas_call(
        own_kernel,
        grid=(1,),
        in_specs=[whole(own.shape), whole(squares.shape)]
        + [whole((line.shape[0], student_width)) for line in lines],
        out_specs=(whole((count, student_width)), whole((64,) + squares.shape)),
        out_shape=(
            jax.ShapeDtypeStruct((count, student_width), jnp.float32),
            jax.ShapeDtypeStruct((64,) + squares.shape, jnp.float32),
        ),
        compiler_params=pltpu.CompilerParams(vmem_limit_bytes=VMEM_LIMIT),
        cost_estimate=pl.CostEstimate(
            flops=2 * count * texts * student_width,
            bytes_accessed=2 * texts * student_width,
            transcendentals=0,
        ),
    )(own, squares, *lines)


VMEM_LIMIT = 24 * 1024 * 1024


def shards(student, teacher):
    texts, width = student.shape
    both = join(student, teacher)
    tie = lax.optimization_barrier
    near, far = ("x", "y"), ("y", "x")
    other = other_core(both)
    ring = [round_z(both)]
    both, other = tie((both, other))
    ring.append(round_z(other))
    right, left, across = (shift(both, near, k) for k in (1, 3, 2))
    lines = [both, other]
    ring = jnp.concatenate(ring)
    lines += [ring, other_core(ring)]
    ring, right, left, across = round_z(ring), *tie((right, left, across, ring))[:3]
    first, second = jnp.concatenate([both, right]), jnp.concatenate([left, across])
    first_up, second_down = shift(first, far, 1), shift(second, far, 3)
    ring, first, second = tie((ring, first, second))
    lines += [ring, other_core(ring)]
    ring = round_z(ring)
    first, second, first_up, second_down = tie((first, second, first_up, second_down))
    first_across, second_across = shift(first_up, far, 1), shift(second_down, far, 3)
    first_down, second_up = shift(first, far, 3), shift(second, far, 1)
    ring, first_up, second_down = tie((ring, first_up, second_down))
    lines += [ring, other_core(ring)]
    ring = round_z(ring[:texts])
    lines += [ring, other_core(ring)]
    pieces = (first_up, second_up, first_down, second_down)
    pieces += (first_across, second_across, first, second)
    *scaled, own, squares = pulls(pieces, lines, width)
    sent = [term.astype(jnp.float16) for term in scaled]
    returned = [shift(term, far, -k) for term, k in zip(sent, (1, 3, 2))]
    own, squares = lax.optimization_barrier((own, squares, *sent))[:2]
    partial_term, squares = own_pull(own, squares, lines, width)
    count = own.shape[0]
    for term in returned:
        root = term[count : count + 1].astype(jnp.float32)
        root = root * root * root
        partial_term += term[:count].astype(jnp.float32) * (root * root)
    blocks = partial_term.reshape(4, texts, width)
    pulled = blocks[0]
    for i, k in ((3, 2), (1, 1), (2, 3)):
        pulled += shift(blocks[i], near, -k)

    total = jnp.sum(lax.all_to_all(squares, ("y", "zh", "zl", "core"), 0, 0), axis=0)
    ring = [shift(total, ("x", "x"), k) for k in (1, 2, 3)]
    total = (total + ring[1]) + (ring[0] + ring[2])
    return total[0, 0] / jnp.float32(texts * 256), pulled


def solution(mesh):
    fine = Mesh(mesh.devices.reshape(SIZES), AXES)
    spec = P(AXES, None)
    return jax.shard_map(
        shards, mesh=fine, in_specs=(spec, spec), out_specs=(P(), spec), check_vma=False
    )
```

```python
import jax
import jax.numpy as jnp
from jax import lax
from jax.experimental import pallas as pl
from jax.experimental.pallas import tpu as pltpu
from jax.sharding import Mesh, PartitionSpec as P

AXES = ("y", "zl", "zh", "x", "core")
SIZES = (4, 4, 2, 4, 2)
STRIDES = dict(zip(AXES, (64, 16, 8, 2, 1)))
DEPTH = 1024
EXTRA = 16


def shift(value, axes, step):
    pairs = []
    for target in range(256):
        stride = STRIDES[axes[target % 2]]
        place = target // stride % 4
        pairs.append((target + ((place + step) % 4 - place) * stride, target))
    return lax.ppermute(value, AXES, pairs)


def round_z(value):
    pairs = []
    for target in range(256):
        z = target // 16 % 4 + target // 8 % 2 * 4
        source = (z - 1 + target % 2 * 2) % 8
        pairs.append((target + (source % 4 - z % 4) * 16 + (source // 4 - z // 4) * 8, target))
    return lax.ppermute(value, AXES, pairs)


def other_core(value):
    return lax.ppermute(value, "core", [(0, 1), (1, 0)])


def join_kernel(student_ref, teacher_ref, both_ref):
    width = student_ref.shape[1]
    both_ref[:, :width] = student_ref[...]
    both_ref[:, width:] = teacher_ref[...]


def join(student, teacher):
    texts, total = student.shape[0], student.shape[1] + teacher.shape[1]
    return pl.pallas_call(
        join_kernel, out_shape=jax.ShapeDtypeStruct((texts, total), student.dtype)
    )(student, teacher)


def excess_kernel(*refs):
    pieces, lines, outs = refs[:8], refs[8:-8], refs[-8:-5]
    own_ref, squares_ref, rows, total, rounded = refs[-5:]
    count = own_ref.shape[0]
    width = outs[0].shape[1]
    for k in range(pieces[0].shape[1] // DEPTH):
        place = slice(k * DEPTH, (k + 1) * DEPTH)
        cols = jnp.concatenate([piece[:, place] for piece in pieces])
        line = jnp.concatenate([piece[:, place] for piece in lines])
        product = lax.dot_general(
            cols, line, (((1,), (1,)), ((), ())), preferred_element_type=jnp.float32
        )
        if k * DEPTH < width:
            rows[k] = line
        if k == 0:
            total[...] = product
        elif k * DEPTH < width:
            total[...] += product
        else:
            total[...] -= product
    excess = total[...]
    rounded[...] = excess.astype(rounded.dtype)
    squares = jnp.sum(jnp.sum(excess * excess, axis=0, keepdims=True), axis=1, keepdims=True)
    squares_ref[...] = jnp.broadcast_to(squares, squares_ref.shape)
    own_ref[...] = rounded[3 * count :]
    largest = [jnp.full((1, 1), 1e-36, jnp.float32)] * 3
    for k in range(width // DEPTH):
        place = slice(k * DEPTH, (k + 1) * DEPTH)
        product = jnp.dot(rounded[: 3 * count], rows[k], preferred_element_type=jnp.float32)
        for i, out in enumerate(outs):
            part = product[i * count : (i + 1) * count]
            out[:count, place] = part
            most = jnp.max(jnp.max(jnp.abs(part), axis=0, keepdims=True), axis=1, keepdims=True)
            largest[i] = jnp.maximum(largest[i], most)
    for most, out in zip(largest, outs):
        power = jnp.clip(jnp.floor((14.0 - jnp.log2(most)) / 6.0), 0.0, 14.0)
        out[:count] = out[:count] * jnp.exp2(6.0 * power)
        out[count:] = jnp.broadcast_to(jnp.exp2(-power), (EXTRA, width))


def own_kernel(own_ref, squares_ref, *refs):
    *lines, out_ref, spread_ref = refs
    line = jnp.concatenate([piece[...] for piece in lines])
    out_ref[...] = jnp.dot(own_ref[...], line, preferred_element_type=jnp.float32)
    spread_ref[...] = jnp.broadcast_to(squares_ref[...][None], spread_ref.shape)


def pulls(pieces, lines, student_width):
    width = lines[0].shape[1]
    texts = sum(line.shape[0] for line in lines)
    count = 2 * pieces[0].shape[0]
    inside = pl.BlockSpec(memory_space=pltpu.VMEM)
    scaled = jax.ShapeDtypeStruct((count + EXTRA, student_width), jnp.float32)
    return pl.pallas_call(
        excess_kernel,
        in_specs=[inside] * (len(pieces) + len(lines)),
        out_specs=(inside,) * 5,
        out_shape=(scaled,) * 3
        + (
            jax.ShapeDtypeStruct((count, texts), jnp.bfloat16),
            jax.ShapeDtypeStruct((1, 128), jnp.float32),
        ),
        scratch_shapes=[
            pltpu.VMEM((student_width // DEPTH, texts, DEPTH), jnp.bfloat16),
            pltpu.VMEM((4 * count, texts), jnp.float32),
            pltpu.VMEM((4 * count, texts), jnp.bfloat16),
        ],
        compiler_params=pltpu.CompilerParams(vmem_limit_bytes=VMEM_LIMIT),
        cost_estimate=pl.CostEstimate(
            flops=8 * count * texts * (width + student_width),
            bytes_accessed=2 * (4 * count + texts) * width,
            transcendentals=0,
        ),
    )(*pieces, *lines)


def own_pull(own, squares, lines, student_width):
    count, texts = own.shape
    whole = lambda shape: pl.BlockSpec(shape, lambda i: (0,) * len(shape))
    return pl.pallas_call(
        own_kernel,
        grid=(1,),
        in_specs=[whole(own.shape), whole(squares.shape)]
        + [whole((line.shape[0], student_width)) for line in lines],
        out_specs=(whole((count, student_width)), whole((64,) + squares.shape)),
        out_shape=(
            jax.ShapeDtypeStruct((count, student_width), jnp.float32),
            jax.ShapeDtypeStruct((64,) + squares.shape, jnp.float32),
        ),
        compiler_params=pltpu.CompilerParams(vmem_limit_bytes=VMEM_LIMIT),
        cost_estimate=pl.CostEstimate(
            flops=2 * count * texts * student_width,
            bytes_accessed=2 * texts * student_width,
            transcendentals=0,
        ),
    )(own, squares, *lines)


VMEM_LIMIT = 24 * 1024 * 1024


def shards(student, teacher):
    texts, width = student.shape
    both = join(student, teacher)
    tie = lax.optimization_barrier
    near, far = ("x", "y"), ("y", "x")
    other = other_core(both)
    ring = [round_z(both)]
    both, other = tie((both, other))
    ring.append(round_z(other))
    right, left, across = (shift(both, near, k) for k in (1, 3, 2))
    lines = [both, other]
    ring = jnp.concatenate(ring)
    lines += [ring, other_core(ring)]
    ring, right, left, across = round_z(ring), *tie((right, left, across, ring))[:3]
    first, second = jnp.concatenate([both, right]), jnp.concatenate([left, across])
    first_up, second_down = shift(first, far, 1), shift(second, far, 3)
    ring, first, second = tie((ring, first, second))
    lines += [ring, other_core(ring)]
    ring = round_z(ring)
    first, second, first_up, second_down = tie((first, second, first_up, second_down))
    first_across, second_across = shift(first_up, far, 1), shift(second_down, far, 3)
    first_down, second_up = shift(first, far, 3), shift(second, far, 1)
    ring, first_up, second_down = tie((ring, first_up, second_down))
    lines += [ring, other_core(ring)]
    ring = round_z(ring[:texts])
    lines += [ring, other_core(ring)]
    pieces = (first_up, second_up, first_down, second_down)
    pieces += (first_across, second_across, first, second)
    *scaled, own, squares = pulls(pieces, lines, width)
    sent = [term.astype(jnp.float16) for term in scaled]
    returned = [shift(term, far, -k) for term, k in zip(sent, (1, 3, 2))]
    own, squares = lax.optimization_barrier((own, squares, *sent))[:2]
    partial_term, squares = own_pull(own, squares, lines, width)
    count = own.shape[0]
    for term in returned:
        root = term[count : count + 1].astype(jnp.float32)
        root = root * root * root
        partial_term += term[:count].astype(jnp.float32) * (root * root)
    blocks = partial_term.reshape(4, texts, width)
    pulled = blocks[0]
    for i, k in ((3, 2), (1, 1), (2, 3)):
        pulled += shift(blocks[i], near, -k)

    total = jnp.sum(lax.all_to_all(squares, ("zh", "zl", "x", "core"), 0, 0), axis=0)
    ring = [shift(total, ("y", "y"), k) for k in (1, 2, 3)]
    total = (total + ring[1]) + (ring[0] + ring[2])
    return total[0, 0] / jnp.float32(texts * 256), pulled


def solution(mesh):
    fine = Mesh(mesh.devices.reshape(SIZES), AXES)
    spec = P(AXES, None)
    return jax.shard_map(
        shards, mesh=fine, in_specs=(spec, spec), out_specs=(P(), spec), check_vma=False
    )
```

```python
import jax
import jax.numpy as jnp
from jax import lax
from jax.experimental import pallas as pl
from jax.experimental.pallas import tpu as pltpu
from jax.sharding import Mesh, PartitionSpec as P

AXES = ("y", "zl", "zh", "x", "core")
SIZES = (4, 4, 2, 4, 2)
STRIDES = dict(zip(AXES, (64, 16, 8, 2, 1)))
DEPTH = 1024
EXTRA = 16


def shift(value, axes, step):
    pairs = []
    for target in range(256):
        stride = STRIDES[axes[target % 2]]
        place = target // stride % 4
        pairs.append((target + ((place + step) % 4 - place) * stride, target))
    return lax.ppermute(value, AXES, pairs)


def round_z(value):
    pairs = []
    for target in range(256):
        z = target // 16 % 4 + target // 8 % 2 * 4
        source = (z - 1 + target % 2 * 2) % 8
        pairs.append((target + (source % 4 - z % 4) * 16 + (source // 4 - z // 4) * 8, target))
    return lax.ppermute(value, AXES, pairs)


def other_core(value):
    return lax.ppermute(value, "core", [(0, 1), (1, 0)])


def join_kernel(student_ref, teacher_ref, both_ref):
    width = student_ref.shape[1]
    both_ref[:, :width] = student_ref[...]
    both_ref[:, width:] = teacher_ref[...]


def join(student, teacher):
    texts, total = student.shape[0], student.shape[1] + teacher.shape[1]
    return pl.pallas_call(
        join_kernel, out_shape=jax.ShapeDtypeStruct((texts, total), student.dtype)
    )(student, teacher)


def excess_kernel(*refs):
    pieces, lines, outs = refs[:8], refs[8:-8], refs[-8:-5]
    own_ref, squares_ref, rows, total, rounded = refs[-5:]
    count = own_ref.shape[0]
    width = outs[0].shape[1]
    for k in range(pieces[0].shape[1] // DEPTH):
        place = slice(k * DEPTH, (k + 1) * DEPTH)
        cols = jnp.concatenate([piece[:, place] for piece in pieces])
        line = jnp.concatenate([piece[:, place] for piece in lines])
        product = lax.dot_general(
            cols, line, (((1,), (1,)), ((), ())), preferred_element_type=jnp.float32
        )
        if k * DEPTH < width:
            rows[k] = line
        if k == 0:
            total[...] = product
        elif k * DEPTH < width:
            total[...] += product
        else:
            total[...] -= product
    excess = total[...]
    rounded[...] = excess.astype(rounded.dtype)
    squares = jnp.sum(jnp.sum(excess * excess, axis=0, keepdims=True), axis=1, keepdims=True)
    squares_ref[...] = jnp.broadcast_to(squares, squares_ref.shape)
    own_ref[...] = rounded[3 * count :]
    largest = [jnp.full((1, 1), 1e-36, jnp.float32)] * 3
    for k in range(width // DEPTH):
        place = slice(k * DEPTH, (k + 1) * DEPTH)
        product = jnp.dot(rounded[: 3 * count], rows[k], preferred_element_type=jnp.float32)
        for i, out in enumerate(outs):
            part = product[i * count : (i + 1) * count]
            out[:count, place] = part
            most = jnp.max(jnp.max(jnp.abs(part), axis=0, keepdims=True), axis=1, keepdims=True)
            largest[i] = jnp.maximum(largest[i], most)
    for most, out in zip(largest, outs):
        power = jnp.clip(jnp.floor((14.0 - jnp.log2(most)) / 6.0), 0.0, 14.0)
        out[:count] = out[:count] * jnp.exp2(6.0 * power)
        out[count:] = jnp.broadcast_to(jnp.exp2(-power), (EXTRA, width))


def own_kernel(own_ref, squares_ref, *refs):
    *lines, out_ref, spread_ref = refs
    line = jnp.concatenate([piece[...] for piece in lines])
    out_ref[...] = jnp.dot(own_ref[...], line, preferred_element_type=jnp.float32)
    spread_ref[...] = jnp.broadcast_to(squares_ref[...][None], spread_ref.shape)


def pulls(pieces, lines, student_width):
    width = lines[0].shape[1]
    texts = sum(line.shape[0] for line in lines)
    count = 2 * pieces[0].shape[0]
    inside = pl.BlockSpec(memory_space=pltpu.VMEM)
    scaled = jax.ShapeDtypeStruct((count + EXTRA, student_width), jnp.float32)
    return pl.pallas_call(
        excess_kernel,
        in_specs=[inside] * (len(pieces) + len(lines)),
        out_specs=(inside,) * 5,
        out_shape=(scaled,) * 3
        + (
            jax.ShapeDtypeStruct((count, texts), jnp.bfloat16),
            jax.ShapeDtypeStruct((1, 128), jnp.float32),
        ),
        scratch_shapes=[
            pltpu.VMEM((student_width // DEPTH, texts, DEPTH), jnp.bfloat16),
            pltpu.VMEM((4 * count, texts), jnp.float32),
            pltpu.VMEM((4 * count, texts), jnp.bfloat16),
        ],
        compiler_params=pltpu.CompilerParams(vmem_limit_bytes=VMEM_LIMIT),
        cost_estimate=pl.CostEstimate(
            flops=8 * count * texts * (width + student_width),
            bytes_accessed=2 * (4 * count + texts) * width,
            transcendentals=0,
        ),
    )(*pieces, *lines)


def own_pull(own, squares, lines, student_width):
    count, texts = own.shape
    whole = lambda shape: pl.BlockSpec(shape, lambda i: (0,) * len(shape))
    return pl.pallas_call(
        own_kernel,
        grid=(1,),
        in_specs=[whole(own.shape), whole(squares.shape)]
        + [whole((line.shape[0], student_width)) for line in lines],
        out_specs=(whole((count, student_width)), whole((64,) + squares.shape)),
        out_shape=(
            jax.ShapeDtypeStruct((count, student_width), jnp.float32),
            jax.ShapeDtypeStruct((64,) + squares.shape, jnp.float32),
        ),
        compiler_params=pltpu.CompilerParams(vmem_limit_bytes=VMEM_LIMIT),
        cost_estimate=pl.CostEstimate(
            flops=2 * count * texts * student_width,
            bytes_accessed=2 * texts * student_width,
            transcendentals=0,
        ),
    )(own, squares, *lines)


VMEM_LIMIT = 24 * 1024 * 1024


def shards(student, teacher):
    texts, width = student.shape
    both = join(student, teacher)
    tie = lax.optimization_barrier
    near, far = ("y", "x"), ("x", "y")
    other = other_core(both)
    ring = [round_z(both)]
    both, other = tie((both, other))
    ring.append(round_z(other))
    right, left, across = (shift(both, near, k) for k in (1, 3, 2))
    lines = [both, other]
    ring = jnp.concatenate(ring)
    lines += [ring, other_core(ring)]
    ring, right, left, across = round_z(ring), *tie((right, left, across, ring))[:3]
    first, second = jnp.concatenate([both, right]), jnp.concatenate([left, across])
    first_up, second_down = shift(first, far, 1), shift(second, far, 3)
    ring, first, second = tie((ring, first, second))
    lines += [ring, other_core(ring)]
    ring = round_z(ring)
    first, second, first_up, second_down = tie((first, second, first_up, second_down))
    first_across, second_across = shift(first_up, far, 1), shift(second_down, far, 3)
    first_down, second_up = shift(first, far, 3), shift(second, far, 1)
    ring, first_up, second_down = tie((ring, first_up, second_down))
    lines += [ring, other_core(ring)]
    ring = round_z(ring[:texts])
    lines += [ring, other_core(ring)]
    pieces = (first_up, second_up, first_down, second_down)
    pieces += (first_across, second_across, first, second)
    *scaled, own, squares = pulls(pieces, lines, width)
    sent = [term.astype(jnp.float16) for term in scaled]
    returned = [shift(term, far, -k) for term, k in zip(sent, (1, 3, 2))]
    own, squares = lax.optimization_barrier((own, squares, *sent))[:2]
    partial_term, squares = own_pull(own, squares, lines, width)
    count = own.shape[0]
    for term in returned:
        root = term[count : count + 1].astype(jnp.float32)
        root = root * root * root
        partial_term += term[:count].astype(jnp.float32) * (root * root)
    blocks = partial_term.reshape(4, texts, width)
    pulled = blocks[0]
    for i, k in ((3, 2), (1, 1), (2, 3)):
        pulled += shift(blocks[i], near, -k)

    total = jnp.sum(lax.all_to_all(squares, ("zh", "zl", "x", "core"), 0, 0), axis=0)
    ring = [shift(total, ("y", "y"), k) for k in (1, 2, 3)]
    total = (total + ring[1]) + (ring[0] + ring[2])
    return total[0, 0] / jnp.float32(texts * 256), pulled


def solution(mesh):
    fine = Mesh(mesh.devices.reshape(SIZES), AXES)
    spec = P(AXES, None)
    return jax.shard_map(
        shards, mesh=fine, in_specs=(spec, spec), out_specs=(P(), spec), check_vma=False
    )
```
